32 devices in a mesh: space: 4 (over z), agg: 8 (over y, x, core).
Axes of the slice: x: 2, y: 2, z: 4, core: 2. Of those that a mesh axis runs over, the one named last changes fastest.
Arguments:
- h_blocks: bfloat16 [4096, 7, 64, 64], P(('space', 'agg')), may hold values from -2.5 to 2.5
- h_cols: int32 [4096, 7], P(('space', 'agg')), may hold values from 0 to 4095, as said below
- p_blocks: bfloat16 [4096, 64, 64], P(('space', 'agg')), may hold values from -0.75 to 0.75
- agg_map: int32 [4096], P(('space', 'agg')), may hold values from 0 to 15, as said below
- term_slot: int32 [4096, 7], P(('space', 'agg')), may hold values from 0 to 6
- owner_pos: int32 [512], P(('space', 'agg')), may hold values from 0 to 511, as said below
Outputs:
- coarse: bfloat16 [512, 7, 64, 64], P(('space', 'agg'))
The draws below stay inside these ranges and needn't reach their ends.
Inputs may be any that keep to these rules, and one draw needn't show every extreme that they name: h_cols[e, 0] = e. Every other entry names an element of the same device, except that for an element among the first 32 of its device (not in the lowest slab) entry 1 names one of the last 32 elements of the device one step lower along space with the same agg index, and for one among the last 32 (not in the highest slab) entry 2 names one of the first 32 elements of the device one step higher along space with the same agg index. `agg_map`: each device's elements form 16 aggregates of exactly 8 elements. `owner_pos`: A permutation of the coarse rows that keeps each space slab: the rows of slab s go to rows s * 128 to (s + 1) * 128 - 1. The owner of output row q is agg index (q % 128) // 16. The 16 rows of one device go to every owner of its slab, exactly 2 to each.
All inputs are finite; a program needn't handle non-finite values.
Results may differ from the reference program's by a relative error of at most 0.0049.
Values may be sent and summed in bfloat16 or wider, within the bound.
A program may use at most 256 MiB of HBM per device.

```python
import jax
import jax.numpy as jnp
from jax import lax

B = 64
K = 7
KC = 7
AGG = 8
E_DEV = 128
FACE = 32
A_DEV = 16
CAP = 2
NA_S = 128
E = 4096
N_SPACE = 4
N_AGG = 8


def draw_h_cols(key, part):
    key = jax.random.fold_in(key, 11)
    keys = jax.random.split(key, 3)
    total = E_DEV * N_SPACE * N_AGG
    rows_all = jnp.arange(total, dtype=jnp.int32)
    device = rows_all // E_DEV
    local = rows_all % E_DEV
    slab = device // N_AGG
    random_local = jax.random.randint(keys[0], (total, K), 0, E_DEV, dtype=jnp.int32)
    columns = device[:, None] * E_DEV + random_local
    columns = columns.at[:, 0].set(rows_all)
    lower_pick = jax.random.randint(keys[1], (total,), E_DEV - FACE, E_DEV, dtype=jnp.int32)
    upper_pick = jax.random.randint(keys[2], (total,), 0, FACE, dtype=jnp.int32)
    use_lower = (local < FACE) & (slab > 0)
    use_upper = (local >= E_DEV - FACE) & (slab < N_SPACE - 1)
    columns = columns.at[:, 1].set(jnp.where(use_lower, (device - N_AGG) * E_DEV + lower_pick, columns[:, 1]))
    columns = columns.at[:, 2].set(jnp.where(use_upper, (device + N_AGG) * E_DEV + upper_pick, columns[:, 2]))
    return columns.astype(jnp.int32)


def draw_agg_map(key, part):
    key = jax.random.fold_in(key, 17)
    devices_all = N_SPACE * N_AGG
    keys = jax.random.split(key, devices_all)
    orders = jax.vmap(lambda sub: jax.random.permutation(sub, E_DEV))(keys)
    return (orders // AGG).reshape(-1).astype(jnp.int32)


def draw_owner_pos(key, part):
    key = jax.random.fold_in(key, 23)
    keys = jax.random.split(key, 2)
    local_keys = jax.random.split(keys[0], N_SPACE * N_AGG)
    local_perm = jax.vmap(lambda sub: jax.random.permutation(sub, A_DEV))(local_keys).reshape(N_SPACE, N_AGG, A_DEV)
    owner_keys = jax.random.split(keys[1], N_SPACE * N_AGG)
    owner_perm = jax.vmap(lambda sub: jax.random.permutation(sub, A_DEV))(owner_keys).reshape(N_SPACE, N_AGG, A_DEV)
    owner = local_perm // CAP
    inside = local_perm % CAP
    source = jnp.arange(N_AGG, dtype=jnp.int32)[None, :, None]
    place = source * CAP + inside
    slab_index = jnp.arange(N_SPACE, dtype=jnp.int32)[:, None, None]
    within = owner_perm[slab_index, owner, place]
    position = slab_index * NA_S + owner * A_DEV + within
    return position.reshape(-1).astype(jnp.int32)


def set_ends(entries, key, least, largest):
    extent = entries.shape
    spot = [jax.random.randint(jax.random.fold_in(key, axis), (), 0, extent[axis]) for axis in range(len(extent))]
    entries = entries.at[tuple(spot)].set(least)
    longest = extent.index(max(extent))
    spot[longest] = (spot[longest] + 1) % extent[longest]
    return entries.at[tuple(spot)].set(largest)


def levels(own_key, dims, shards, low, top_value):
    def one(dim, blocks):
        draws = jax.random.uniform(jax.random.fold_in(jax.random.fold_in(own_key, 6), dim), (blocks,), jnp.float32, low / len(shards), top_value / len(shards))
        return jnp.repeat(jnp.exp(draws), dims[dim] // blocks).reshape((-1,) + (1,) * (len(dims) - dim - 1))

    gain = one(*shards[0])
    for cut in shards[1:]:
        gain = gain * one(*cut)
    return gain


def gaussian(stream_key, extent, scale, bound, cuts=(), kind=jnp.bfloat16):
    factor_of = levels(stream_key, extent, cuts, -0.22, 0.18) if cuts else 1.0
    entries = jax.random.normal(stream_key, extent, jnp.float32) * scale * factor_of
    return jnp.minimum(jnp.maximum(entries, -bound), bound).astype(kind)


def setup_inputs(seed: int = 0) -> dict:
    key_list = jax.random.split(jax.random.key(seed), 7)
    return {
        "h_blocks": gaussian(key_list[0], (E, K, B, B), 0.35, 2.5, ((0, 32),)),
        "h_cols": draw_h_cols(jax.random.fold_in(key_list[6], 71), 0),
        "p_blocks": gaussian(key_list[2], (E, B, B), B ** -0.5, 0.75, ((0, 32),)),
        "agg_map": draw_agg_map(jax.random.fold_in(key_list[6], 71), 0),
        "term_slot": set_ends(jax.random.randint(key_list[4], (E, K), 0, KC), jax.random.fold_in(key_list[4], 1), 0, KC - 1).astype(jnp.int32),
        "owner_pos": draw_owner_pos(jax.random.fold_in(key_list[6], 71), 0),
    }


def reference(h_blocks, h_cols, p_blocks, agg_map, term_slot, owner_pos):
    total = h_blocks.shape[0]
    blocks_count = total // E_DEV
    h_split = h_blocks.reshape(blocks_count, E_DEV, K, B, B)
    col_split = h_cols.reshape(blocks_count, E_DEV, K)
    p_split = p_blocks.reshape(blocks_count, E_DEV, B, B)
    agg_split = agg_map.reshape(blocks_count, E_DEV)
    slot_split = term_slot.reshape(blocks_count, E_DEV, K)

    def one_block(items):
        h_here, cols_here, p_here, agg_here, slot_here = items
        gathered = jnp.take(p_blocks, cols_here.astype(jnp.int32), axis=0)
        hp_part = jnp.einsum("ekij,ekjl->ekil", h_here.astype(jnp.float32), gathered.astype(jnp.float32)).astype(jnp.bfloat16)
        terms = jnp.einsum("eji,ekjl->ekil", p_here.astype(jnp.float32), hp_part.astype(jnp.float32))
        target = (agg_here[:, None] * KC + slot_here).astype(jnp.int32).reshape(-1)
        summed = jax.ops.segment_sum(terms.reshape(E_DEV * K, B, B), target, num_segments=A_DEV * KC)
        return summed.reshape(A_DEV, KC, B, B).astype(jnp.bfloat16)

    rowsum = lax.map(one_block, (h_split, col_split, p_split, agg_split, slot_split))
    rowsum = rowsum.reshape(blocks_count * A_DEV, KC, B, B)
    coarse = jnp.zeros_like(rowsum).at[owner_pos.astype(jnp.int32)].set(rowsum)
    return coarse
```

```python
import functools

import jax
import jax.numpy as jnp
from jax import lax
from jax.experimental import pallas as pl
from jax.experimental.pallas import tpu as pltpu
from jax.sharding import PartitionSpec as P

KC = 7
VMEM_LIMIT = 48 * 1024 * 1024


def pair_kernel(x_ref, o_ref, turned):
    _, rows, cols, elems = x_ref.shape
    half = rows // 2
    for q in range(half):
        both = jnp.concatenate([x_ref[0, q], x_ref[0, half + q]], axis=0)
        turned[pl.ds(q * elems, elems), :] = both.T.astype(jnp.float32)
    for e in range(elems):
        o_ref[e, 0] = turned[pl.ds(e, half, stride=elems), :].astype(o_ref.dtype)


def paired(x):
    count, rows, cols, elems = x.shape
    half = rows // 2
    return pl.pallas_call(
        pair_kernel,
        grid=(count,),
        in_specs=[pl.BlockSpec((1, rows, cols, elems), lambda k: (k, 0, 0, 0))],
        out_specs=pl.BlockSpec((elems, 1, half, 2 * cols), lambda k: (0, k, 0, 0)),
        out_shape=jax.ShapeDtypeStruct((elems, count, half, 2 * cols), x.dtype),
        scratch_shapes=[pltpu.VMEM((half * elems, 2 * cols), jnp.float32)],
        compiler_params=pltpu.CompilerParams(vmem_limit_bytes=VMEM_LIMIT),
        cost_estimate=pl.CostEstimate(flops=0, bytes_accessed=4 * x.size, transcendentals=0),
    )(x)


def swap_halves(x):
    half = x.shape[-1] // 2
    return jnp.concatenate([x[:, half:], x[:, :half]], axis=1)


def galerkin_kernel(n_agg, dev_ref, cols_ref, slot_ref, agg_ref, owner_ref,
                    h_ref, before_ref, own_ref, after_ref, o_ref,
                    dense, stack, total, order, place, count):
    step = pl.program_id(0)
    elems = own_ref.shape[0]
    face = before_ref.shape[0]
    half, lanes = own_ref.shape[1:]
    size = lanes // 2
    aggs = owner_ref.shape[0]
    per_agg = elems // aggs
    cap = aggs // n_agg
    low = lax.broadcasted_iota(jnp.int32, (half, lanes), 1) < size
    low2 = lax.broadcasted_iota(jnp.int32, (size, lanes), 1) < size

    @pl.when(step == 0)
    def _():
        def clear(i, c):
            count[i] = 0
            return c
        lax.fori_loop(0, aggs + n_agg, clear, 0)

        def rank_row(r, c):
            owner = lax.rem(owner_ref[r], aggs * n_agg) // aggs
            seen = count[aggs + owner]
            count[aggs + owner] = seen + 1
            place[r] = owner * cap + seen
            return c
        lax.fori_loop(0, aggs, rank_row, 0)

        def rank_elem(e, c):
            a = agg_ref[e]
            seen = count[a]
            count[a] = seen + 1
            order[place[a] * per_agg + seen] = e
            return c
        lax.fori_loop(0, elems, rank_elem, 0)

        def spread(src, first):
            def one(c, carry):
                x = src[c].astype(jnp.float32)
                y = swap_halves(x)
                dense[first + c, 0:half] = jnp.where(low, x, 0.0).astype(jnp.bfloat16)
                dense[first + c, half:2 * half] = jnp.where(low, y, 0.0).astype(jnp.bfloat16)
                dense[first + c, 2 * half:3 * half] = jnp.where(low, 0.0, y).astype(jnp.bfloat16)
                dense[first + c, 3 * half:4 * half] = jnp.where(low, 0.0, x).astype(jnp.bfloat16)
                return carry
            lax.fori_loop(0, src.shape[0], one, 0, unroll=4)
        spread(before_ref, 0)
        spread(own_ref, face)
        spread(after_ref, face + elems)

    dev = dev_ref[0]
    base = dev * elems
    hop = n_agg * elems
    total[...] = jnp.zeros_like(total)
    for t in range(per_agg):
        e = order[step * per_agg + t]
        stack[pl.ds(t * half, half), :] = own_ref[e]
        for k in range(KC):
            x = cols_ref[k, e] - base
            c = jnp.where(x < 0, x + hop - (elems - face),
                          jnp.where(x >= elems, x - hop + face + elems, x + face))
            hp = jnp.dot(h_ref[e, k], dense[c], preferred_element_type=jnp.float32)
            total[slot_ref[k, e], pl.ds(t * half, half), :] += hp
    left = stack[...].T
    for j in range(0, KC, 2):
        if j + 1 < KC:
            right = jnp.concatenate([total[j], total[j + 1]], axis=1).astype(jnp.bfloat16)
        else:
            right = total[j].astype(jnp.bfloat16)
        r = jnp.dot(left, right, preferred_element_type=jnp.float32)
        a_top, a_bot = r[:size, :lanes], r[size:, :lanes]
        if j + 1 < KC:
            b_top, b_bot = r[:size, lanes:], r[size:, lanes:]
        else:
            b_top = b_bot = jnp.zeros_like(a_top)
        out = jnp.where(low2, a_top, b_bot) + swap_halves(jnp.where(low2, b_top, a_bot))
        o_ref[0, j // 2] = out.astype(o_ref.dtype)


def galerkin(n_agg, dev, cols, slots, agg_map, owner_pos, h, before, own, after):
    elems, _, half, lanes = h.shape
    face = before.shape[0]
    aggs = owner_pos.shape[0]
    smem = pl.BlockSpec(memory_space=pltpu.SMEM)
    vmem = pl.BlockSpec(memory_space=pltpu.VMEM)
    tiles = (KC + 1) // 2
    return pl.pallas_call(
        functools.partial(galerkin_kernel, n_agg),
        grid=(aggs,),
        in_specs=[smem] * 5 + [vmem] * 4,
        out_specs=pl.BlockSpec((1, tiles, lanes // 2, lanes), lambda g: (g, 0, 0, 0)),
        out_shape=jax.ShapeDtypeStruct((aggs, tiles, lanes // 2, lanes), jnp.bfloat16),
        scratch_shapes=[
            pltpu.VMEM((elems + 2 * face, lanes, lanes), jnp.bfloat16),
            pltpu.VMEM((elems // aggs * half, lanes), jnp.bfloat16),
            pltpu.VMEM((KC, elems // aggs * half, lanes), jnp.float32),
            pltpu.SMEM((elems,), jnp.int32),
            pltpu.SMEM((aggs,), jnp.int32),
            pltpu.SMEM((aggs + n_agg,), jnp.int32),
        ],
        compiler_params=pltpu.CompilerParams(vmem_limit_bytes=VMEM_LIMIT),
    )(dev, cols, slots, agg_map, owner_pos, h, before, own, after)


def place_kernel(n_agg, me_ref, owner_ref, x_ref, o_ref, source, count):
    rows, tiles, size, lanes = x_ref.shape
    cap = rows // n_agg
    me = me_ref[0]

    def one(i, seen):
        spot = lax.rem(owner_ref[i], rows * n_agg)
        mine = spot // rows == me

        @pl.when(mine)
        def _():
            source[lax.rem(spot, rows)] = seen
        return seen + mine.astype(jnp.int32)
    lax.fori_loop(0, rows * n_agg, one, 0)

    def row(q, carry):
        s = source[q]
        for t in range(tiles):
            x = x_ref[s, t]
            o_ref[q, 2 * t] = x[:, :size]
            if 2 * t + 1 < KC:
                o_ref[q, 2 * t + 1] = x[:, size:]
        return carry
    lax.fori_loop(0, rows, row, 0)


def placed_rows(n_agg, me, owners, x):
    rows, tiles, size, lanes = x.shape
    return pl.pallas_call(
        functools.partial(place_kernel, n_agg),
        in_specs=[pl.BlockSpec(memory_space=pltpu.SMEM)] * 2 + [pl.BlockSpec(memory_space=pltpu.VMEM)],
        out_specs=pl.BlockSpec(memory_space=pltpu.VMEM),
        out_shape=jax.ShapeDtypeStruct((rows, KC, size, size), x.dtype),
        scratch_shapes=[pltpu.SMEM((rows,), jnp.int32), pltpu.SMEM((1,), jnp.int32)],
        compiler_params=pltpu.CompilerParams(vmem_limit_bytes=VMEM_LIMIT),
    )(me, owners, x)


def body(h_blocks, h_cols, p_blocks, agg_map, term_slot, owner_pos):
    elems = p_blocks.shape[0]
    face = elems // 4
    aggs = owner_pos.shape[0]
    n_agg = lax.axis_size("agg")
    n_space = lax.axis_size("space")
    me = lax.axis_index("agg")
    device = lax.axis_index("space") * n_agg + me
    owners = lax.all_gather(owner_pos, "agg", tiled=True)

    own = paired(p_blocks.transpose(1, 2, 0)[None])[:, 0]
    up = [(i, i + 1) for i in range(n_space - 1)]
    down = [(j, i) for i, j in up]
    before = lax.ppermute(own[elems - face:], "space", up)
    after = lax.ppermute(own[:face], "space", down)
    h = paired(h_blocks.transpose(1, 2, 3, 0))
    rows = galerkin(n_agg, device.reshape(1).astype(jnp.int32), h_cols.T, term_slot.T,
                    agg_map, owner_pos, h, before, own, after)
    tail = rows.shape[1:]
    got = lax.all_to_all(rows.reshape((n_agg, aggs // n_agg) + tail), "agg", 0, 0)
    return placed_rows(n_agg, me.reshape(1).astype(jnp.int32), owners, got.reshape((aggs,) + tail))


def solution(mesh):
    placed = (
        P(("space", "agg"), None, None, None),
        P(("space", "agg"), None),
        P(("space", "agg"), None, None),
        P(("space", "agg")),
        P(("space", "agg"), None),
        P(("space", "agg")),
    )
    return jax.shard_map(
        body,
        mesh=mesh,
        in_specs=placed,
        out_specs=P(("space", "agg"), None, None, None),
        check_vma=False,
    )
```

```python
import functools

import jax
import jax.numpy as jnp
from jax import lax
from jax.experimental import pallas as pl
from jax.experimental.pallas import tpu as pltpu
from jax.sharding import PartitionSpec as P

KC = 7
VMEM_LIMIT = 24 * 1024 * 1024
PREPARE_VMEM = 52 * 1024 * 1024
PITCH = 8


def turn(blocks, store, turned):
    rows, _, elems = blocks.shape
    half = rows // 2
    pitch = elems + PITCH
    for q in range(half):
        both = jnp.concatenate([blocks[q], blocks[half + q]], axis=0)
        turned[pl.ds(q * pitch, elems), :] = both.T.astype(jnp.float32)
    for e in range(elems):
        store(e, turned[pl.ds(e, half, stride=pitch), :].astype(jnp.bfloat16))


def pair_kernel(x_ref, o_ref, turned):
    def store(e, block):
        o_ref[e] = block
    turn(x_ref, store, turned)


def paired(x):
    rows, cols, elems = x.shape
    half = rows // 2
    return pl.pallas_call(
        pair_kernel,
        in_specs=[pl.BlockSpec(memory_space=pltpu.VMEM)],
        out_specs=pl.BlockSpec(memory_space=pltpu.VMEM),
        out_shape=jax.ShapeDtypeStruct((elems, half, 2 * cols), x.dtype),
        scratch_shapes=[pltpu.VMEM((half * (elems + PITCH), 2 * cols), jnp.float32)],
        compiler_params=pltpu.CompilerParams(vmem_limit_bytes=VMEM_LIMIT),
    )(x)


def prepare_kernel(n_agg, agg_ref, owner_ref, h_ref, o_ref, order, within,
                   raw, turned, place, count, sems):
    for k in range(KC):
        pltpu.make_async_copy(h_ref.at[k], raw.at[k], sems.at[k]).start()
    elems = agg_ref.shape[0]
    aggs = owner_ref.shape[0]
    per_agg = elems // aggs
    cap = aggs // n_agg
    for i in range(aggs + n_agg):
        count[i] = 0

    def rank_row(r, c):
        spot = lax.rem(owner_ref[r], aggs * n_agg)
        owner = spot // aggs
        seen = count[aggs + owner]
        count[aggs + owner] = seen + 1
        spot_rank = owner * cap + seen
        place[r] = spot_rank * per_agg
        within[spot_rank] = spot - owner * aggs
        return c
    lax.fori_loop(0, aggs, rank_row, 0, unroll=4)

    def rank_elem(e, c):
        a = agg_ref[e]
        seen = place[a]
        place[a] = seen + 1
        order[seen] = e
        return c
    lax.fori_loop(0, elems, rank_elem, 0, unroll=8)

    def one(k, c):
        pltpu.make_async_copy(h_ref.at[k], raw.at[k], sems.at[k]).wait()

        def store(e, block):
            o_ref[e, k] = block
        turn(raw.at[k], store, turned)
        return c
    lax.fori_loop(0, KC, one, 0)


def prepare(n_agg, agg_map, owner_pos, x):
    count, rows, cols, elems = x.shape
    half = rows // 2
    aggs = owner_pos.shape[0]
    smem = pl.BlockSpec(memory_space=pltpu.SMEM)
    vmem = pl.BlockSpec(memory_space=pltpu.VMEM)
    return pl.pallas_call(
        functools.partial(prepare_kernel, n_agg),
        in_specs=[smem, smem, pl.BlockSpec(memory_space=pl.ANY)],
        out_specs=(vmem, smem, smem),
        out_shape=(
            jax.ShapeDtypeStruct((elems, count, half, 2 * cols), x.dtype),
            jax.ShapeDtypeStruct((elems,), jnp.int32),
            jax.ShapeDtypeStruct((aggs,), jnp.int32),
        ),
        scratch_shapes=[
            pltpu.VMEM(x.shape, x.dtype),
            pltpu.VMEM((half * (elems + PITCH), 2 * cols), jnp.float32),
            pltpu.SMEM((aggs,), jnp.int32),
            pltpu.SMEM((aggs + n_agg,), jnp.int32),
            pltpu.SemaphoreType.DMA((count,)),
        ],
        compiler_params=pltpu.CompilerParams(vmem_limit_bytes=PREPARE_VMEM),
        cost_estimate=pl.CostEstimate(flops=0, bytes_accessed=4 * x.size, transcendentals=0),
    )(agg_map, owner_pos, x)


def swap_halves(x):
    half = x.shape[-1] // 2
    return jnp.concatenate([x[:, half:], x[:, :half]], axis=1)


def galerkin_kernel(n_agg, dev_ref, cols_ref, slot_ref, order, within,
                    h_ref, before_ref, own_ref, after_ref, o_ref, dense, stack, total):
    elems = own_ref.shape[0]
    face = before_ref.shape[0]
    half, lanes = own_ref.shape[1:]
    size = lanes // 2
    groups = within.shape[0]
    per_agg = elems // groups
    low = lax.broadcasted_iota(jnp.int32, (half, lanes), 1) < size
    low2 = lax.broadcasted_iota(jnp.int32, (size, lanes), 1) < size

    def spread(src, first):
        def one(c, carry):
            x = src[c]
            y = swap_halves(x)
            zero = jnp.zeros_like(x)
            dense[first + c, 0:half] = jnp.where(low, x, zero)
            dense[first + c, half:2 * half] = jnp.where(low, y, zero)
            dense[first + c, 2 * half:3 * half] = jnp.where(low, zero, y)
            dense[first + c, 3 * half:4 * half] = jnp.where(low, zero, x)
            return carry
        lax.fori_loop(0, src.shape[0], one, 0, unroll=8)
    spread(before_ref, 0)
    spread(own_ref, face)
    spread(after_ref, face + elems)

    dev = dev_ref[0]
    base = dev * elems
    hop = n_agg * elems

    def group(g, carry):
        total[...] = jnp.zeros_like(total)
        for t in range(per_agg):
            e = order[g * per_agg + t]
            stack[pl.ds(t * half, half), :] = own_ref[e]
            for k in range(KC):
                x = cols_ref[k, e] - base
                c = jnp.where(x < 0, x + hop - (elems - face),
                              jnp.where(x >= elems, x - hop + face + elems, x + face))
                hp = jnp.dot(h_ref[e, k], dense[c], preferred_element_type=jnp.float32)
                total[slot_ref[k, e], pl.ds(t * half, half), :] += hp
        left = stack[...].T
        for j in range(0, KC, 2):
            if j + 1 < KC:
                right = jnp.concatenate([total[j], total[j + 1]], axis=1).astype(jnp.bfloat16)
            else:
                right = total[j].astype(jnp.bfloat16)
            r = jnp.dot(left, right, preferred_element_type=jnp.float32)
            a_top, a_bot = r[:size, :lanes], r[size:, :lanes]
            if j + 1 < KC:
                b_top, b_bot = r[:size, lanes:], r[size:, lanes:]
                out = jnp.where(low2, a_top, b_bot) + swap_halves(jnp.where(low2, b_top, a_bot))
            else:
                out = jnp.where(low2, a_top + swap_halves(a_bot), within[g].astype(jnp.float32))
            o_ref[g, j // 2] = out.astype(o_ref.dtype)
        return carry
    lax.fori_loop(0, groups, group, 0)


def galerkin(n_agg, dev, cols, slots, order, within, h, before, own, after):
    elems, _, half, lanes = h.shape
    face = before.shape[0]
    aggs = within.shape[0]
    smem = pl.BlockSpec(memory_space=pltpu.SMEM)
    vmem = pl.BlockSpec(memory_space=pltpu.VMEM)
    tiles = (KC + 1) // 2
    return pl.pallas_call(
        functools.partial(galerkin_kernel, n_agg),
        in_specs=[smem] * 5 + [vmem] * 4,
        out_specs=vmem,
        out_shape=jax.ShapeDtypeStruct((aggs, tiles, lanes // 2, lanes), jnp.bfloat16),
        scratch_shapes=[
            pltpu.VMEM((elems + 2 * face, lanes, lanes), jnp.bfloat16),
            pltpu.VMEM((elems // aggs * half, lanes), jnp.bfloat16),
            pltpu.VMEM((KC, elems // aggs * half, lanes), jnp.float32),
        ],
        compiler_params=pltpu.CompilerParams(vmem_limit_bytes=VMEM_LIMIT),
    )(dev, cols, slots, order, within, h, before, own, after)


def place_kernel(x_ref, o_ref, spots):
    rows, tiles, size, lanes = x_ref.shape
    high = lax.broadcasted_iota(jnp.int32, (16, lanes), 1) >= lanes // 2
    for s in range(rows):
        mark = jnp.where(high, x_ref[s, tiles - 1, 0:16].astype(jnp.float32), 0.0)
        spots[s] = jnp.max(mark).astype(jnp.int32)

    def row(s, carry):
        q = spots[s]
        for t in range(tiles):
            x = x_ref[s, t]
            o_ref[q, 2 * t] = x[:, :size]
            if 2 * t + 1 < KC:
                o_ref[q, 2 * t + 1] = x[:, size:]
        return carry
    lax.fori_loop(0, rows, row, 0, unroll=2)


def placed_rows(x):
    rows, tiles, size, lanes = x.shape
    return pl.pallas_call(
        place_kernel,
        in_specs=[pl.BlockSpec(memory_space=pltpu.VMEM)],
        out_specs=pl.BlockSpec(memory_space=pltpu.VMEM),
        out_shape=jax.ShapeDtypeStruct((rows, KC, size, size), x.dtype),
        scratch_shapes=[pltpu.SMEM((rows,), jnp.int32)],
        compiler_params=pltpu.CompilerParams(vmem_limit_bytes=VMEM_LIMIT),
    )(x)


def body(h_blocks, h_cols, p_blocks, agg_map, term_slot, owner_pos):
    elems = p_blocks.shape[0]
    face = elems // 4
    aggs = owner_pos.shape[0]
    n_agg = lax.axis_size("agg")
    n_space = lax.axis_size("space")
    device = lax.axis_index("space") * n_agg + lax.axis_index("agg")

    own = paired(p_blocks.transpose(1, 2, 0))
    up = [(i, i + 1) for i in range(n_space - 1)]
    down = [(j, i) for i, j in up]
    before = lax.ppermute(own[elems - face:], "space", up)
    after = lax.ppermute(own[:face], "space", down)
    h, order, within = prepare(n_agg, agg_map, owner_pos, h_blocks.transpose(1, 2, 3, 0))
    rows = galerkin(n_agg, device.reshape(1).astype(jnp.int32), h_cols.T, term_slot.T,
                    order, within, h, before, own, after)
    tail = rows.shape[1:]
    got = lax.all_to_all(rows.reshape((n_agg, aggs // n_agg) + tail), "agg", 0, 0)
    return placed_rows(got.reshape((aggs,) + tail))


def solution(mesh):
    placed = (
        P(("space", "agg"), None, None, None),
        P(("space", "agg"), None),
        P(("space", "agg"), None, None),
        P(("space", "agg")),
        P(("space", "agg"), None),
        P(("space", "agg")),
    )
    return jax.shard_map(
        body,
        mesh=mesh,
        in_specs=placed,
        out_specs=P(("space", "agg"), None, None, None),
        check_vma=False,
    )
```

```python
import functools

import jax
import jax.numpy as jnp
from jax import lax
from jax.experimental import pallas as pl
from jax.experimental.pallas import tpu as pltpu
from jax.sharding import PartitionSpec as P

KC = 7
VMEM_LIMIT = 24 * 1024 * 1024
PREPARE_VMEM = 45 * 1024 * 1024
PITCH = 8


def turn(blocks, store, turned):
    rows, _, elems = blocks.shape
    half = rows // 2
    pitch = elems + PITCH
    for q in range(half):
        both = jnp.concatenate([blocks[q], blocks[half + q]], axis=0)
        turned[pl.ds(q * pitch, elems), :] = both.T.astype(jnp.float32)
    for e in range(elems):
        store(e, turned[pl.ds(e, half, stride=pitch), :].astype(jnp.bfloat16))


def sort_and_pair_kernel(n_agg, agg_ref, owner_ref, p_ref, o_ref, order, within,
                         raw, turned, place, count, sem):
    copy = pltpu.make_async_copy(p_ref, raw, sem)
    copy.start()
    elems = agg_ref.shape[0]
    aggs = owner_ref.shape[0]
    per_agg = elems // aggs
    cap = aggs // n_agg
    for i in range(n_agg):
        count[i] = i * cap

    def rank_row(r, c):
        spot = lax.rem(owner_ref[r], aggs * n_agg)
        owner = spot // aggs
        rank = count[owner]
        count[owner] = rank + 1
        place[r] = rank * per_agg
        within[rank] = spot - owner * aggs
        return c
    lax.fori_loop(0, aggs, rank_row, 0, unroll=4)

    def rank_elem(e, c):
        a = agg_ref[e]
        seen = place[a]
        place[a] = seen + 1
        order[seen] = e
        return c
    lax.fori_loop(0, elems, rank_elem, 0, unroll=8)
    copy.wait()

    def store(e, block):
        o_ref[e] = block
    turn(raw, store, turned)


def sort_and_pair(n_agg, agg_map, owner_pos, x):
    rows, cols, elems = x.shape
    half = rows // 2
    aggs = owner_pos.shape[0]
    smem = pl.BlockSpec(memory_space=pltpu.SMEM)
    vmem = pl.BlockSpec(memory_space=pltpu.VMEM)
    return pl.pallas_call(
        functools.partial(sort_and_pair_kernel, n_agg),
        in_specs=[smem, smem, pl.BlockSpec(memory_space=pl.ANY)],
        out_specs=(vmem, smem, smem),
        out_shape=(
            jax.ShapeDtypeStruct((elems, half, 2 * cols), x.dtype),
            jax.ShapeDtypeStruct((elems,), jnp.int32),
            jax.ShapeDtypeStruct((aggs,), jnp.int32),
        ),
        scratch_shapes=[
            pltpu.VMEM(x.shape, x.dtype),
            pltpu.VMEM((half * (elems + PITCH), 2 * cols), jnp.float32),
            pltpu.SMEM((aggs,), jnp.int32),
            pltpu.SMEM((n_agg,), jnp.int32),
            pltpu.SemaphoreType.DMA,
        ],
        compiler_params=pltpu.CompilerParams(vmem_limit_bytes=PREPARE_VMEM),
    )(agg_map, owner_pos, x)


def prepare_kernel(h_ref, own_ref, o_ref, before_ref, after_ref,
                   raw, turned, sems, up_sems, down_sems):
    for k in range(KC):
        pltpu.make_async_copy(h_ref.at[k], raw.at[k], sems.at[k]).start()
    slab = lax.axis_index("space")
    slabs = lax.axis_size("space")
    elems = own_ref.shape[0]
    face = before_ref.shape[0]
    lower, upper = slab > 0, slab < slabs - 1
    barrier = pltpu.get_barrier_semaphore()

    def upward():
        return pltpu.make_async_remote_copy(
            src_ref=own_ref.at[pl.ds(elems - face, face)], dst_ref=before_ref,
            send_sem=up_sems.at[0], recv_sem=up_sems.at[1],
            device_id={"space": slab + 1}, device_id_type=pl.DeviceIdType.MESH)

    def downward():
        return pltpu.make_async_remote_copy(
            src_ref=own_ref.at[pl.ds(0, face)], dst_ref=after_ref,
            send_sem=down_sems.at[0], recv_sem=down_sems.at[1],
            device_id={"space": slab - 1}, device_id_type=pl.DeviceIdType.MESH)

    @pl.when(upper)
    def _():
        pl.semaphore_signal(barrier, inc=1, device_id={"space": slab + 1},
                            device_id_type=pl.DeviceIdType.MESH)

    @pl.when(lower)
    def _():
        pl.semaphore_signal(barrier, inc=1, device_id={"space": slab - 1},
                            device_id_type=pl.DeviceIdType.MESH)

    def one(k, c):
        pltpu.make_async_copy(h_ref.at[k], raw.at[k], sems.at[k]).wait()

        def store(e, block):
            o_ref[e, k] = block
        turn(raw.at[k], store, turned)
        return c
    lax.fori_loop(0, 1, one, 0)
    pl.semaphore_wait(barrier, lower.astype(jnp.int32) + upper.astype(jnp.int32))

    @pl.when(upper)
    def _():
        upward().start()

    @pl.when(lower)
    def _():
        downward().start()
    lax.fori_loop(1, KC, one, 0)

    @pl.when(upper)
    def _():
        upward().wait_send()
        downward().wait_recv()

    @pl.when(lower)
    def _():
        downward().wait_send()
        upward().wait_recv()

    @pl.when(jnp.logical_not(upper))
    def _():
        after_ref[...] = jnp.zeros_like(after_ref)

    @pl.when(jnp.logical_not(lower))
    def _():
        before_ref[...] = jnp.zeros_like(before_ref)


def prepare(x, own):
    count, rows, cols, elems = x.shape
    half = rows // 2
    face = elems // 4
    vmem = pl.BlockSpec(memory_space=pltpu.VMEM)
    edge = jax.ShapeDtypeStruct((face, half, 2 * cols), x.dtype)
    return pl.pallas_call(
        prepare_kernel,
        in_specs=[pl.BlockSpec(memory_space=pl.ANY), vmem],
        out_specs=(vmem, vmem, vmem),
        out_shape=(jax.ShapeDtypeStruct((elems, count, half, 2 * cols), x.dtype), edge, edge),
        scratch_shapes=[
            pltpu.VMEM(x.shape, x.dtype),
            pltpu.VMEM((half * (elems + PITCH), 2 * cols), jnp.float32),
            pltpu.SemaphoreType.DMA((count,)),
            pltpu.SemaphoreType.DMA((2,)),
            pltpu.SemaphoreType.DMA((2,)),
        ],
        compiler_params=pltpu.CompilerParams(
            vmem_limit_bytes=PREPARE_VMEM, collective_id=0, has_side_effects=True),
    )(x, own)


def exchange_kernel(n_agg, x_ref, o_ref, send_sems, recv_sems, local_sem):
    cap = x_ref.shape[0] // n_agg
    me = lax.axis_index("agg")
    barrier = pltpu.get_barrier_semaphore()
    for d in range(1, n_agg):
        pl.semaphore_signal(barrier, inc=1, device_id={"agg": lax.rem(me + d, n_agg)},
                            device_id_type=pl.DeviceIdType.MESH)
    mine = pl.ds(me * cap, cap)
    local = pltpu.make_async_copy(x_ref.at[mine], o_ref.at[mine], local_sem)
    local.start()
    pl.semaphore_wait(barrier, n_agg - 1)
    copies = []
    for d in range(1, n_agg):
        peer = lax.rem(me + d, n_agg)
        copy = pltpu.make_async_remote_copy(
            src_ref=x_ref.at[pl.ds(peer * cap, cap)], dst_ref=o_ref.at[mine],
            send_sem=send_sems.at[d], recv_sem=recv_sems.at[d],
            device_id={"agg": peer}, device_id_type=pl.DeviceIdType.MESH)
        copy.start()
        copies.append(copy)
    local.wait()
    for copy in copies:
        copy.wait()


def exchanged(n_agg, x):
    vmem = pl.BlockSpec(memory_space=pltpu.VMEM)
    return pl.pallas_call(
        functools.partial(exchange_kernel, n_agg),
        in_specs=[vmem],
        out_specs=vmem,
        out_shape=jax.ShapeDtypeStruct(x.shape, x.dtype),
        scratch_shapes=[
            pltpu.SemaphoreType.DMA((n_agg,)),
            pltpu.SemaphoreType.DMA((n_agg,)),
            pltpu.SemaphoreType.DMA,
        ],
        compiler_params=pltpu.CompilerParams(
            vmem_limit_bytes=VMEM_LIMIT, collective_id=1, has_side_effects=True),
    )(x)


def swap_halves(x):
    half = x.shape[-1] // 2
    return jnp.concatenate([x[:, half:], x[:, :half]], axis=1)


def galerkin_kernel(n_agg, dev_ref, cols_ref, slot_ref, order, within,
                    h_ref, before_ref, own_ref, after_ref, o_ref, dense, stack, total):
    elems = own_ref.shape[0]
    face = before_ref.shape[0]
    half, lanes = own_ref.shape[1:]
    size = lanes // 2
    groups = within.shape[0]
    per_agg = elems // groups
    low = lax.broadcasted_iota(jnp.int32, (half, lanes), 1) < size
    low2 = lax.broadcasted_iota(jnp.int32, (size, lanes), 1) < size

    def spread(src, first):
        def one(c, carry):
            x = src[c]
            y = swap_halves(x)
            zero = jnp.zeros_like(x)
            dense[first + c, 0:half] = jnp.where(low, x, zero)
            dense[first + c, half:2 * half] = jnp.where(low, y, zero)
            dense[first + c, 2 * half:3 * half] = jnp.where(low, zero, y)
            dense[first + c, 3 * half:4 * half] = jnp.where(low, zero, x)
            return carry
        lax.fori_loop(0, src.shape[0], one, 0, unroll=8)
    spread(before_ref, 0)
    spread(own_ref, face)
    spread(after_ref, face + elems)

    dev = dev_ref[0]
    base = dev * elems
    hop = n_agg * elems

    def group(g, carry):
        total[...] = jnp.zeros_like(total)
        for t in range(per_agg):
            e = order[g * per_agg + t]
            stack[pl.ds(t * half, half), :] = own_ref[e]
            for k in range(KC):
                x = cols_ref[k, e] - base
                c = jnp.where(x < 0, x + hop - (elems - face),
                              jnp.where(x >= elems, x - hop + face + elems, x + face))
                hp = jnp.dot(h_ref[e, k], dense[c], preferred_element_type=jnp.float32)
                total[slot_ref[k, e], pl.ds(t * half, half), :] += hp
        left = stack[...].T
        for j in range(0, KC, 2):
            if j + 1 < KC:
                right = jnp.concatenate([total[j], total[j + 1]], axis=1).astype(jnp.bfloat16)
            else:
                right = total[j].astype(jnp.bfloat16)
            r = jnp.dot(left, right, preferred_element_type=jnp.float32)
            a_top, a_bot = r[:size, :lanes], r[size:, :lanes]
            if j + 1 < KC:
                b_top, b_bot = r[:size, lanes:], r[size:, lanes:]
                out = jnp.where(low2, a_top, b_bot) + swap_halves(jnp.where(low2, b_top, a_bot))
            else:
                out = jnp.where(low2, a_top + swap_halves(a_bot), within[g].astype(jnp.float32))
            o_ref[g, j // 2] = out.astype(o_ref.dtype)
        return carry
    lax.fori_loop(0, groups, group, 0)


def galerkin(n_agg, dev, cols, slots, order, within, h, before, own, after):
    elems, _, half, lanes = h.shape
    face = before.shape[0]
    aggs = within.shape[0]
    smem = pl.BlockSpec(memory_space=pltpu.SMEM)
    vmem = pl.BlockSpec(memory_space=pltpu.VMEM)
    tiles = (KC + 1) // 2
    return pl.pallas_call(
        functools.partial(galerkin_kernel, n_agg),
        in_specs=[smem] * 5 + [vmem] * 4,
        out_specs=vmem,
        out_shape=jax.ShapeDtypeStruct((aggs, tiles, lanes // 2, lanes), jnp.bfloat16),
        scratch_shapes=[
            pltpu.VMEM((elems + 2 * face, lanes, lanes), jnp.bfloat16),
            pltpu.VMEM((elems // aggs * half, lanes), jnp.bfloat16),
            pltpu.VMEM((KC, elems // aggs * half, lanes), jnp.float32),
        ],
        compiler_params=pltpu.CompilerParams(vmem_limit_bytes=VMEM_LIMIT),
    )(dev, cols, slots, order, within, h, before, own, after)


def place_kernel(x_ref, o_ref, spots):
    rows, tiles, size, lanes = x_ref.shape
    high = lax.broadcasted_iota(jnp.int32, (16, lanes), 1) >= lanes // 2
    for s in range(rows):
        mark = jnp.where(high, x_ref[s, tiles - 1, 0:16].astype(jnp.float32), 0.0)
        spots[s] = jnp.max(mark).astype(jnp.int32)

    def row(s, carry):
        q = spots[s]
        for t in range(tiles):
            x = x_ref[s, t]
            o_ref[q, 2 * t] = x[:, :size]
            if 2 * t + 1 < KC:
                o_ref[q, 2 * t + 1] = x[:, size:]
        return carry
    lax.fori_loop(0, rows, row, 0, unroll=2)


def placed_rows(x):
    rows, tiles, size, lanes = x.shape
    return pl.pallas_call(
        place_kernel,
        in_specs=[pl.BlockSpec(memory_space=pltpu.VMEM)],
        out_specs=pl.BlockSpec(memory_space=pltpu.VMEM),
        out_shape=jax.ShapeDtypeStruct((rows, KC, size, size), x.dtype),
        scratch_shapes=[pltpu.SMEM((rows,), jnp.int32)],
        compiler_params=pltpu.CompilerParams(vmem_limit_bytes=VMEM_LIMIT),
    )(x)


def body(h_blocks, h_cols, p_blocks, agg_map, term_slot, owner_pos):
    n_agg = lax.axis_size("agg")
    device = lax.axis_index("space") * n_agg + lax.axis_index("agg")
    own, order, within = sort_and_pair(n_agg, agg_map, owner_pos, p_blocks.transpose(1, 2, 0))
    h, before, after = prepare(h_blocks.transpose(1, 2, 3, 0), own)
    rows = galerkin(n_agg, device.reshape(1).astype(jnp.int32), h_cols.T, term_slot.T,
                    order, within, h, before, own, after)
    return placed_rows(exchanged(n_agg, rows))


def solution(mesh):
    placed = (
        P(("space", "agg"), None, None, None),
        P(("space", "agg"), None),
        P(("space", "agg"), None, None),
        P(("space", "agg")),
        P(("space", "agg"), None),
        P(("space", "agg")),
    )
    return jax.shard_map(
        body,
        mesh=mesh,
        in_specs=placed,
        out_specs=P(("space", "agg"), None, None, None),
        check_vma=False,
    )
```

```python
import functools

import jax
import jax.numpy as jnp
from jax import lax
from jax.experimental import pallas as pl
from jax.experimental.pallas import tpu as pltpu
from jax.sharding import PartitionSpec as P

KC = 7
VMEM_LIMIT = 24 * 1024 * 1024
PREPARE_VMEM = 45 * 1024 * 1024
PITCH = 8


def turn(blocks, store, turned):
    rows, _, elems = blocks.shape
    half = rows // 2
    pitch = elems + PITCH
    for q in range(half):
        both = jnp.concatenate([blocks[q], blocks[half + q]], axis=0)
        turned[pl.ds(q * pitch, elems), :] = both.T.astype(jnp.float32)
    for e in range(elems):
        store(e, turned[pl.ds(e, half, stride=pitch), :].astype(jnp.bfloat16))


def sort_and_pair_kernel(n_agg, agg_ref, owner_ref, p_ref, o_ref, order, within,
                         raw, turned, place, count, sem):
    copy = pltpu.make_async_copy(p_ref, raw, sem)
    copy.start()
    elems = agg_ref.shape[0]
    aggs = owner_ref.shape[0]
    per_agg = elems // aggs
    cap = aggs // n_agg
    for i in range(n_agg):
        count[i] = i * cap

    def rank_row(r, c):
        spot = lax.rem(owner_ref[r], aggs * n_agg)
        owner = spot // aggs
        rank = count[owner]
        count[owner] = rank + 1
        place[r] = rank * per_agg
        within[rank] = spot - owner * aggs
        return c
    lax.fori_loop(0, aggs, rank_row, 0, unroll=4)

    def rank_elem(e, c):
        a = agg_ref[e]
        seen = place[a]
        place[a] = seen + 1
        order[seen] = e
        return c
    lax.fori_loop(0, elems, rank_elem, 0, unroll=8)
    copy.wait()

    def store(e, block):
        o_ref[e] = block
    turn(raw, store, turned)


def sort_and_pair(n_agg, agg_map, owner_pos, x):
    rows, cols, elems = x.shape
    half = rows // 2
    aggs = owner_pos.shape[0]
    smem = pl.BlockSpec(memory_space=pltpu.SMEM)
    vmem = pl.BlockSpec(memory_space=pltpu.VMEM)
    return pl.pallas_call(
        functools.partial(sort_and_pair_kernel, n_agg),
        in_specs=[smem, smem, pl.BlockSpec(memory_space=pl.ANY)],
        out_specs=(vmem, smem, smem),
        out_shape=(
            jax.ShapeDtypeStruct((elems, half, 2 * cols), x.dtype),
            jax.ShapeDtypeStruct((elems,), jnp.int32),
            jax.ShapeDtypeStruct((aggs,), jnp.int32),
        ),
        scratch_shapes=[
            pltpu.VMEM(x.shape, x.dtype),
            pltpu.VMEM((half * (elems + PITCH), 2 * cols), jnp.float32),
            pltpu.SMEM((aggs,), jnp.int32),
            pltpu.SMEM((n_agg,), jnp.int32),
            pltpu.SemaphoreType.DMA,
        ],
        compiler_params=pltpu.CompilerParams(vmem_limit_bytes=PREPARE_VMEM),
    )(agg_map, owner_pos, x)


def prepare_kernel(h_ref, own_ref, o_ref, before_ref, after_ref,
                   raw, turned, sems, up_sems, down_sems):
    for k in range(KC):
        pltpu.make_async_copy(h_ref.at[k], raw.at[k], sems.at[k]).start()
    slab = lax.axis_index("space")
    slabs = lax.axis_size("space")
    elems = own_ref.shape[0]
    face = before_ref.shape[0]
    lower, upper = slab > 0, slab < slabs - 1
    barrier = pltpu.get_barrier_semaphore()

    def upward():
        return pltpu.make_async_remote_copy(
            src_ref=own_ref.at[pl.ds(elems - face, face)], dst_ref=before_ref,
            send_sem=up_sems.at[0], recv_sem=up_sems.at[1],
            device_id={"space": slab + 1}, device_id_type=pl.DeviceIdType.MESH)

    def downward():
        return pltpu.make_async_remote_copy(
            src_ref=own_ref.at[pl.ds(0, face)], dst_ref=after_ref,
            send_sem=down_sems.at[0], recv_sem=down_sems.at[1],
            device_id={"space": slab - 1}, device_id_type=pl.DeviceIdType.MESH)

    @pl.when(upper)
    def _():
        pl.semaphore_signal(barrier, inc=1, device_id={"space": slab + 1},
                            device_id_type=pl.DeviceIdType.MESH)

    @pl.when(lower)
    def _():
        pl.semaphore_signal(barrier, inc=1, device_id={"space": slab - 1},
                            device_id_type=pl.DeviceIdType.MESH)

    def one(k, c):
        pltpu.make_async_copy(h_ref.at[k], raw.at[k], sems.at[k]).wait()

        def store(e, block):
            o_ref[e, k] = block
        turn(raw.at[k], store, turned)
        return c
    lax.fori_loop(0, 1, one, 0)
    pl.semaphore_wait(barrier, lower.astype(jnp.int32) + upper.astype(jnp.int32))

    @pl.when(upper)
    def _():
        upward().start()

    @pl.when(lower)
    def _():
        downward().start()
    lax.fori_loop(1, KC, one, 0)

    @pl.when(upper)
    def _():
        upward().wait_send()
        downward().wait_recv()

    @pl.when(lower)
    def _():
        downward().wait_send()
        upward().wait_recv()

    @pl.when(jnp.logical_not(upper))
    def _():
        after_ref[...] = jnp.zeros_like(after_ref)

    @pl.when(jnp.logical_not(lower))
    def _():
        before_ref[...] = jnp.zeros_like(before_ref)


def prepare(x, own):
    count, rows, cols, elems = x.shape
    half = rows // 2
    face = elems // 4
    vmem = pl.BlockSpec(memory_space=pltpu.VMEM)
    edge = jax.ShapeDtypeStruct((face, half, 2 * cols), x.dtype)
    return pl.pallas_call(
        prepare_kernel,
        in_specs=[pl.BlockSpec(memory_space=pl.ANY), vmem],
        out_specs=(vmem, vmem, vmem),
        out_shape=(jax.ShapeDtypeStruct((elems, count, half, 2 * cols), x.dtype), edge, edge),
        scratch_shapes=[
            pltpu.VMEM(x.shape, x.dtype),
            pltpu.VMEM((half * (elems + PITCH), 2 * cols), jnp.float32),
            pltpu.SemaphoreType.DMA((count,)),
            pltpu.SemaphoreType.DMA((2,)),
            pltpu.SemaphoreType.DMA((2,)),
        ],
        compiler_params=pltpu.CompilerParams(
            vmem_limit_bytes=PREPARE_VMEM, collective_id=0, has_side_effects=True),
    )(x, own)


def swap_halves(x):
    half = x.shape[-1] // 2
    return jnp.concatenate([x[:, half:], x[:, :half]], axis=1)


def galerkin_kernel(n_agg, dev_ref, cols_ref, slot_ref, order, within,
                    h_ref, before_ref, own_ref, after_ref, o_ref,
                    dense, stack, sums, rows, send_sems, recv_sems):
    elems = own_ref.shape[0]
    face = before_ref.shape[0]
    half, lanes = own_ref.shape[1:]
    size = lanes // 2
    groups = within.shape[0]
    per_agg = elems // groups
    cap = groups // n_agg
    me = lax.axis_index("agg")
    mesh_id = pl.DeviceIdType.MESH
    barrier = pltpu.get_barrier_semaphore()
    for d in range(1, n_agg):
        pl.semaphore_signal(barrier, inc=1, device_id={"agg": lax.rem(me + d, n_agg)}, device_id_type=mesh_id)
    low = lax.broadcasted_iota(jnp.int32, (half, lanes), 1) < size
    low2 = lax.broadcasted_iota(jnp.int32, (size, lanes), 1) < size

    def spread(src, first):
        def one(c, carry):
            x = src[c]
            y = swap_halves(x)
            zero = jnp.zeros_like(x)
            dense[first + c, 0:half] = jnp.where(low, x, zero)
            dense[first + c, half:2 * half] = jnp.where(low, y, zero)
            dense[first + c, 2 * half:3 * half] = jnp.where(low, zero, y)
            dense[first + c, 3 * half:4 * half] = jnp.where(low, zero, x)
            return carry
        lax.fori_loop(0, src.shape[0], one, 0, unroll=8)
    spread(before_ref, 0)
    spread(own_ref, face)
    spread(after_ref, face + elems)

    dev = dev_ref[0]
    base = dev * elems
    hop = n_agg * elems

    def group(g, out_ref):
        for t in range(per_agg):
            e = order[g * per_agg + t]
            part = pl.ds(t * half, half)
            stack[part, :] = own_ref[e]
            slots = [None] * KC
            for k in range(KC):
                x = cols_ref[k, e] - base
                c = jnp.where(x < 0, x + hop - (elems - face),
                              jnp.where(x >= elems, x - hop + face + elems, x + face))
                hp = jnp.dot(h_ref[e, k], dense[c], preferred_element_type=jnp.float32)
                slot = slot_ref[k, e]
                for j in range(KC):
                    own_part = hp * jnp.where(slot == j, 1.0, 0.0)
                    slots[j] = own_part if k == 0 else slots[j] + own_part
            for j in range(KC):
                sums[part, j * lanes:(j + 1) * lanes] = slots[j].astype(jnp.bfloat16)
        left = stack[...].T
        for j in range(0, KC, 2):
            wide = min(2, KC - j) * lanes
            r = jnp.dot(left, sums[:, j * lanes:j * lanes + wide], preferred_element_type=jnp.float32)
            a_top, a_bot = r[:size, :lanes], r[size:, :lanes]
            if j + 1 < KC:
                b_top, b_bot = r[:size, lanes:], r[size:, lanes:]
                out = jnp.where(low2, a_top, b_bot) + swap_halves(jnp.where(low2, b_top, a_bot))
            else:
                out = jnp.where(low2, a_top + swap_halves(a_bot), within[g].astype(jnp.float32))
            out_ref[g, j // 2] = out.astype(o_ref.dtype)

    def sending(i):
        peer = lax.rem(me + 1 + i, n_agg)
        return pltpu.make_async_remote_copy(
            src_ref=rows.at[pl.ds(peer * cap, cap)], dst_ref=o_ref.at[pl.ds(me * cap, cap)],
            send_sem=send_sems.at[i], recv_sem=recv_sems.at[i],
            device_id={"agg": peer}, device_id_type=mesh_id)

    def to_owner(i, carry):
        peer = lax.rem(me + 1 + i, n_agg)

        def one(c, inner):
            group(peer * cap + c, rows)
            return inner
        lax.fori_loop(0, cap, one, 0)
        sending(i).start()
        return carry
    pl.semaphore_wait(barrier, n_agg - 1)
    lax.fori_loop(0, n_agg - 1, to_owner, 0)

    def one(c, inner):
        group(me * cap + c, o_ref)
        return inner
    lax.fori_loop(0, cap, one, 0)
    for i in range(n_agg - 1):
        sending(i).wait()


def galerkin(n_agg, dev, cols, slots, order, within, h, before, own, after):
    elems, _, half, lanes = h.shape
    face = before.shape[0]
    aggs = within.shape[0]
    smem = pl.BlockSpec(memory_space=pltpu.SMEM)
    vmem = pl.BlockSpec(memory_space=pltpu.VMEM)
    tiles = (KC + 1) // 2
    return pl.pallas_call(
        functools.partial(galerkin_kernel, n_agg),
        in_specs=[smem] * 5 + [vmem] * 4,
        out_specs=vmem,
        out_shape=jax.ShapeDtypeStruct((aggs, tiles, lanes // 2, lanes), jnp.bfloat16),
        scratch_shapes=[
            pltpu.VMEM((elems + 2 * face, lanes, lanes), jnp.bfloat16),
            pltpu.VMEM((elems // aggs * half, lanes), jnp.bfloat16),
            pltpu.VMEM((elems // aggs * half, KC * lanes), jnp.bfloat16),
            pltpu.VMEM((aggs, tiles, lanes // 2, lanes), jnp.bfloat16),
            pltpu.SemaphoreType.DMA((n_agg,)),
            pltpu.SemaphoreType.DMA((n_agg,)),
        ],
        compiler_params=pltpu.CompilerParams(
            vmem_limit_bytes=VMEM_LIMIT, collective_id=1, has_side_effects=True),
    )(dev, cols, slots, order, within, h, before, own, after)


def place_kernel(x_ref, o_ref, spots):
    rows, tiles, size, lanes = x_ref.shape
    high = lax.broadcasted_iota(jnp.int32, (16, lanes), 1) >= lanes // 2
    for s in range(rows):
        mark = jnp.where(high, x_ref[s, tiles - 1, 0:16].astype(jnp.float32), 0.0)
        spots[s] = jnp.max(mark).astype(jnp.int32)

    def row(s, carry):
        q = spots[s]
        for t in range(tiles):
            x = x_ref[s, t]
            o_ref[q, 2 * t] = x[:, :size]
            if 2 * t + 1 < KC:
                o_ref[q, 2 * t + 1] = x[:, size:]
        return carry
    lax.fori_loop(0, rows, row, 0, unroll=2)


def placed_rows(x):
    rows, tiles, size, lanes = x.shape
    return pl.pallas_call(
        place_kernel,
        in_specs=[pl.BlockSpec(memory_space=pltpu.VMEM)],
        out_specs=pl.BlockSpec(memory_space=pltpu.VMEM),
        out_shape=jax.ShapeDtypeStruct((rows, KC, size, size), x.dtype),
        scratch_shapes=[pltpu.SMEM((rows,), jnp.int32)],
        compiler_params=pltpu.CompilerParams(vmem_limit_bytes=VMEM_LIMIT),
    )(x)


def body(h_blocks, h_cols, p_blocks, agg_map, term_slot, owner_pos):
    n_agg = lax.axis_size("agg")
    device = lax.axis_index("space") * n_agg + lax.axis_index("agg")
    own, order, within = sort_and_pair(n_agg, agg_map, owner_pos, p_blocks.transpose(1, 2, 0))
    h, before, after = prepare(h_blocks.transpose(1, 2, 3, 0), own)
    rows = galerkin(n_agg, device.reshape(1).astype(jnp.int32), h_cols.T, term_slot.T,
                    order, within, h, before, own, after)
    return placed_rows(rows)


def solution(mesh):
    placed = (
        P(("space", "agg"), None, None, None),
        P(("space", "agg"), None),
        P(("space", "agg"), None, None),
        P(("space", "agg")),
        P(("space", "agg"), None),
        P(("space", "agg")),
    )
    return jax.shard_map(
        body,
        mesh=mesh,
        in_specs=placed,
        out_specs=P(("space", "agg"), None, None, None),
        check_vma=False,
    )
```
